32 devices in a mesh: groups: 2 (over y), span: 4 (over z), section: 2 (over x), mp: 2 (over core).
Axes of the slice: x: 2, y: 2, z: 4, core: 2. Of those that a mesh axis runs over, the one named last changes fastest.
Arguments:
- activations: bfloat16 [2, 2560, 3072], P('section', ('groups', 'span'), 'mp'), parts along dimension 1, may hold values from -6 to 6
- projected: bfloat16 [2, 3, 2560, 3072], P('section', None, ('groups', 'span'), 'mp'), parts along dimension 2, may hold values from -6 to 6
- noise_levels: int32 [2, 8], P('section', ('groups', 'span')), parts along dimension 1, may hold values from 0 to 15
- frame_counts: int32 [2, 8], P('section', 'groups'), parts along dimension 1, may hold values from 1 to 16, as said below
- span_mask: int32 [8, 4], P('groups'), parts along dimension 0, may hold values from 0 to 1, as said below
- gates: float32 [2, 16, 3072], P('section', None, 'mp'), may hold values from -4 to 4
- norm_gains: float32 [2, 2, 24, 128], P('section', None, 'mp'), may hold values from 1.2 to 2
Outputs:
- handed: bfloat16 [2, 2560, 3072], P('section', ('groups', 'span'), 'mp'), parts along dimension 1
The draws below stay inside these ranges and needn't reach their ends.
There are 2 independent parts, one for each index of `groups`. The reference program is written for one: setup_inputs(seed, part) draws one part's arguments, and reference() takes and returns one part's arrays. A program takes and returns all parts, laid end to end along the dimension named above; an argument that names none is the same for every part. Nothing has to cross between parts.
Inputs may be any that keep to these rules, and one draw needn't show every extreme that they name: `frame_counts`: some entry equals 16 and some entry equals 1. span_mask[c][c] = 1; span_mask[c][j] = 0 where j > c or j < c - 2; some row c has span_mask[c][c - 2] = 1.
All inputs are finite; a program needn't handle non-finite values.
Results may differ from the reference program's by a relative error of at most 0.0046.
Values may be sent and summed in bfloat16 or wider, within the bound.
A program may use at most 64 MiB of HBM per device.

```python
import math
import jax
import jax.numpy as jnp
from jax import lax

HEADS = 24
HEAD_DIM = 128
FRAMES = 16
TPF = 20
LEVELS = 16
WIN = 2
TC = 320
SPANS = 4
TOKENS = 1280
SECTIONS = 2
FEAT = 3072


def draw_frame_counts(key, part):
    first, second, third = jax.random.split(key, 3)
    total_cells = SECTIONS * SPANS
    counts = jax.random.randint(first, (total_cells,), 1, FRAMES + 1)
    top_cell = jax.random.randint(second, (), 0, total_cells)
    low_cell = (top_cell + 1 + jax.random.randint(third, (), 0, total_cells - 1)) % total_cells
    cell_ids = jnp.arange(total_cells)
    counts = jnp.where(cell_ids == top_cell, FRAMES, counts)
    counts = jnp.where(cell_ids == low_cell, 1, counts)
    return counts.reshape(SECTIONS, SPANS).astype(jnp.int32)


def draw_span_mask(key, part):
    first, second = jax.random.split(key)
    row_ids = jnp.arange(SPANS)[:, None]
    col_ids = jnp.arange(SPANS)[None, :]
    lag_spans = row_ids - col_ids
    coins = jax.random.randint(first, (SPANS, SPANS), 0, 5) < 3
    forced_row = jax.random.randint(second, (), WIN, SPANS)
    forced = (row_ids == forced_row) & (lag_spans == WIN)
    inside = (lag_spans >= 1) & (lag_spans <= WIN)
    chosen = jnp.where(lag_spans == 0, 1, jnp.where(inside & (coins | forced), 1, 0))
    return chosen.astype(jnp.int32)


def place_ends(result, stream_key, low, top_value):
    longest = result.shape.index(max(result.shape))
    spots = []
    for shift in (0, 1):
        where = [jax.random.randint(jax.random.fold_in(stream_key, axis), (), 0, length) for axis, length in enumerate(result.shape)]
        where[longest] = (where[longest] + shift) % result.shape[longest]
        spots.append(tuple(where))
    return result.at[spots[0]].set(low).at[spots[1]].set(top_value)


def block_scale(key, shape, cuts, low, high):
    factor_of = 1.0
    for dim, parts in cuts:
        steps = jax.random.uniform(jax.random.fold_in(jax.random.fold_in(key, 6), dim), (parts,), jnp.float32, low / len(cuts), high / len(cuts))
        factor_of = factor_of * jnp.repeat(jnp.exp(steps), shape[dim] // parts).reshape((-1,) + (1,) * (len(shape) - 1 - dim))
    return factor_of


def gaussian(key, extent, deviation, reach, cuts=(), kind=jnp.bfloat16):
    result = jax.random.normal(key, extent, jnp.float32) * deviation
    if len(cuts) > 0:
        result = block_scale(key, extent, cuts, -0.22, 0.18) * result
    return jnp.clip(result, min=-reach, max=reach).astype(kind)


def setup_inputs(seed: int = 0, part: int = 0) -> dict:
    key_of = jax.random.split(jax.random.key(seed), 8)
    part_keys = jax.random.split(jax.random.fold_in(key_of[7], part), 8)
    return {
        "activations": gaussian(part_keys[0], (SECTIONS, TOKENS, FEAT), 1.0, 6.0, ((0, 2), (1, 4), (2, 2))),
        "projected": gaussian(part_keys[1], (SECTIONS, 3, TOKENS, FEAT), 1.0, 6.0, ((0, 2), (2, 4), (3, 2))),
        "noise_levels": place_ends(jax.random.randint(part_keys[2], (SECTIONS, SPANS), 0, LEVELS), jax.random.fold_in(part_keys[2], 1), 0, LEVELS - 1).astype(jnp.int32),
        "frame_counts": draw_frame_counts(jax.random.fold_in(jax.random.fold_in(key_of[7], part), 71), part),
        "span_mask": draw_span_mask(jax.random.fold_in(jax.random.fold_in(key_of[7], part), 71), part),
        "gates": gaussian(key_of[5], (SECTIONS, LEVELS, FEAT), 1.0, 4.0, ((0, 2), (2, 2)), jnp.float32),
        "norm_gains": jnp.clip(1.2 + 0.79999995 * jax.random.uniform(key_of[6], (SECTIONS, 2, HEADS, HEAD_DIM), jnp.float32) ** block_scale(key_of[6], (SECTIONS, 2, HEADS, HEAD_DIM), ((0, 2), (2, 2)), -0.2, 0.2), 1.2, 2.0),
    }


EPSILON = 1e-06

def normalize(values, gain_row):
    mean_square = lax.optimization_barrier(jnp.mean(values * values, axis=-1, keepdims=True))
    return values * lax.rsqrt(mean_square + EPSILON) * gain_row

def reference(activations, projected, noise_levels, frame_counts, span_mask, gates, norm_gains):
    token_frame = jnp.arange(TC, dtype=jnp.int32) // TPF
    layer_outs = []
    for section in range(SECTIONS):
        stream = activations[section].astype(jnp.float32)
        inputs = projected[section].reshape(3, SPANS, TC, HEADS, HEAD_DIM)
        query_vecs = normalize(inputs[0].astype(jnp.float32), norm_gains[section, 0]).astype(jnp.bfloat16)
        key_vecs = normalize(inputs[1].astype(jnp.float32), norm_gains[section, 1]).astype(jnp.bfloat16)
        value_vecs = inputs[2]
        onehot = (jnp.arange(LEVELS, dtype=jnp.int32)[None, :] == noise_levels[section][:, None]).astype(jnp.float32)
        gate_rows = jnp.einsum('cl,lf->cf', onehot, gates[section], precision=lax.Precision.HIGHEST)
        valid = (token_frame[None, :] < frame_counts[section][:, None]).astype(jnp.float32)
        key_weight = span_mask.astype(jnp.float32)[:, :, None] * valid[None, :, :]
        padded_weight = jnp.concatenate([jnp.zeros((SPANS, WIN, TC), jnp.float32), key_weight], axis=1)
        pad_keys = jnp.zeros((WIN, TC, HEADS, HEAD_DIM), jnp.bfloat16)
        padded_keys = jnp.concatenate([pad_keys, key_vecs], axis=0)
        padded_values = jnp.concatenate([pad_keys, value_vecs], axis=0)

        def attend(index):
            query_rows = lax.dynamic_index_in_dim(query_vecs, index, 0, keepdims=False)
            keys_win = lax.dynamic_slice_in_dim(padded_keys, index, WIN + 1, 0).reshape((WIN + 1) * TC, HEADS, HEAD_DIM)
            values_win = lax.dynamic_slice_in_dim(padded_values, index, WIN + 1, 0).reshape((WIN + 1) * TC, HEADS, HEAD_DIM)
            weight_row = lax.dynamic_index_in_dim(padded_weight, index, 0, keepdims=False)
            weight_win = lax.dynamic_slice_in_dim(weight_row, index, WIN + 1, 0).reshape((WIN + 1) * TC)
            scores = jnp.einsum('qhe,khe->hqk', query_rows.astype(jnp.float32), keys_win.astype(jnp.float32)) / math.sqrt(HEAD_DIM)
            exp_scores = jnp.exp(scores) * weight_win[None, None, :]
            weight_sum = lax.optimization_barrier(jnp.sum(exp_scores, axis=-1))
            soft_weights = lax.optimization_barrier(exp_scores.astype(jnp.bfloat16))
            numerator = jnp.einsum('hqk,khe->qhe', soft_weights.astype(jnp.float32), values_win.astype(jnp.float32))
            return numerator / jnp.transpose(weight_sum)[:, :, None]
        attended = lax.map(attend, jnp.arange(SPANS, dtype=jnp.int32)).reshape(SPANS, TC, FEAT)
        gated_out = (attended * gate_rows[:, None, :]).reshape(TOKENS, FEAT)
        layer_outs.append((stream + gated_out).astype(jnp.bfloat16))
    return jnp.roll(jnp.stack(layer_outs), 1, axis=0)
```

```python
import functools
import math

import jax
import jax.numpy as jnp
from jax import lax
from jax.experimental import pallas as pl
from jax.experimental.pallas import tpu as pltpu
from jax.sharding import PartitionSpec as P

FRAMES = 16
EPSILON = 1e-06
MESH = pl.DeviceIdType.MESH
SPLIT = 2
RELAY_LAG, FAR_LAG, NEAR_LAG, OWN_LAG = 1, 2, 4, 6
MASKED = -1e30


def normalize(values, gain_row):
    values = values.astype(jnp.float32)
    mean_square = jnp.mean(values * values, axis=-1, keepdims=True)
    return (values * lax.rsqrt(mean_square + EPSILON) * gain_row).astype(jnp.bfloat16)


def kernel(
    spans, sections, steps,
    act_ref, proj_ref, noise_ref, count_ref, mask_ref, gate_ref, gain_ref,
    out_ref,
    q_own, keys, vals, q_next, q_far, far_out, far_sum, far_in, far_sum_in,
    near_out, near_sum, near_in, near_sum_in, done,
    s_own, r_own, s_rel, r_rel, s_far, r_far, s_fars, r_fars,
    s_near, r_near, s_nears, r_nears, s_out, r_out,
):
    me = lax.axis_index("span")
    section = lax.axis_index("section")
    has_prev = me > 0
    has_next = me < spans - 1
    has_far = me < spans - 2
    prev_id = {"span": jnp.maximum(me - 1, 0)}
    next_id = {"span": jnp.minimum(me + 1, spans - 1)}
    out_id = {"section": lax.rem(section + 1, sections)}
    in_id = {"section": lax.rem(section + sections - 1, sections)}

    tokens = act_ref.shape[1]
    heads = gain_ref.shape[2]
    size = gain_ref.shape[3]
    rows = tokens // SPLIT
    scale = math.log2(math.e) / math.sqrt(size)
    tiles = [(lo, min(size, rows - lo)) for lo in range(0, rows, size)]

    barrier = pltpu.get_barrier_semaphore()
    pl.semaphore_signal(barrier, inc=1, device_id=out_id, device_id_type=MESH)
    pl.semaphore_signal(barrier, inc=1, device_id=in_id, device_id_type=MESH)

    @pl.when(has_prev)
    def _():
        pl.semaphore_signal(barrier, inc=1, device_id=prev_id, device_id_type=MESH)

    @pl.when(has_next)
    def _():
        pl.semaphore_signal(barrier, inc=1, device_id=next_id, device_id_type=MESH)

    token_row = lax.broadcasted_iota(jnp.int32, (1, tokens), 1)
    valid = token_row < count_ref[0, me] * (tokens // FRAMES)

    def bias_of(distance):
        allowed = mask_ref[jnp.minimum(me + distance, spans - 1), me]
        return jnp.where(valid & (allowed > 0), 0.0, MASKED)

    eye = lax.broadcasted_iota(jnp.int32, (size, size), 0) == lax.broadcasted_iota(
        jnp.int32, (size, size), 1
    )

    def lanes(head):
        return pl.ds(pl.multiple_of(head * size, size), size)

    def prepare(head):
        keys[head] = normalize(
            proj_ref[0, 1, :, lanes(head)], gain_ref[0, 1, pl.ds(head, 1), :]
        )
        vals[head, :, :size] = proj_ref[0, 2, :, lanes(head)]
        vals[head, :, size:] = jnp.ones((tokens, size), jnp.bfloat16)
        query = normalize(
            proj_ref[0, 0, :, lanes(head)], gain_ref[0, 0, pl.ds(head, 1), :]
        )
        for part in range(SPLIT):
            q_own[head * SPLIT + part] = query[part * rows:(part + 1) * rows]

    @pl.loop(0, heads)
    def _(head):
        prepare(head)

    def attend(query, head, bias):
        scores = lax.dot_general(
            query, keys[head], (((1,), (1,)), ((), ())),
            preferred_element_type=jnp.float32,
        )
        weights = jnp.exp2(scores * scale + bias).astype(jnp.bfloat16)
        both = jnp.dot(weights, vals[head], preferred_element_type=jnp.float32)
        return both[:, :size], both[:, size:]

    def put_sum(ref, index, total):
        for n, (lo, length) in enumerate(tiles):
            picked = jnp.where(eye[:length], total[lo:lo + length], 0.0)
            ref[index, :, n * size:(n + 1) * size] = jnp.sum(picked, axis=0, keepdims=True)

    def get_sum(ref, index):
        columns = []
        for n, (lo, length) in enumerate(tiles):
            row = ref[index, :, n * size:(n + 1) * size]
            picked = jnp.where(eye[:length], row, 0.0)
            columns.append(jnp.sum(picked, axis=1, keepdims=True))
        return jnp.concatenate(columns, axis=0)

    def copy(src, dst, send, recv, index, where):
        return pltpu.make_async_remote_copy(
            src_ref=src.at[index], dst_ref=dst.at[index],
            send_sem=send.at[index], recv_sem=recv.at[index],
            device_id=where, device_id_type=MESH,
        )

    def own_copy(i):
        return copy(q_own, q_next, s_own, r_own, i, prev_id)

    def relay_copy(i):
        return copy(q_next, q_far, s_rel, r_rel, i, prev_id)

    def far_copies(i):
        return (copy(far_out, far_in, s_far, r_far, i, next_id),
                copy(far_sum, far_sum_in, s_fars, r_fars, i, next_id))

    def near_copies(i):
        return (copy(near_out, near_in, s_near, r_near, i, next_id),
                copy(near_sum, near_sum_in, s_nears, r_nears, i, next_id))

    def out_copy(i):
        head, part = i // SPLIT, i % SPLIT
        place = pl.ds(pl.multiple_of(part * rows, rows), rows)
        return pltpu.make_async_remote_copy(
            src_ref=done.at[i], dst_ref=out_ref.at[0, place, lanes(head)],
            send_sem=s_out.at[i], recv_sem=r_out.at[i],
            device_id=out_id, device_id_type=MESH,
        )

    pl.semaphore_wait(
        barrier, 2 + has_prev.astype(jnp.int32) + has_next.astype(jnp.int32)
    )

    level = noise_ref[0, 0]
    bias_own, bias_near, bias_far = bias_of(0), bias_of(1), bias_of(2)

    @pl.loop(0, steps + OWN_LAG)
    def _(step):
        @pl.when((step < steps) & has_prev)
        def _():
            own_copy(step).start()

        relay = step - RELAY_LAG

        @pl.when((relay >= 0) & (relay < steps) & has_next)
        def _():
            own_copy(relay).wait_recv()

            @pl.when(has_prev)
            def _():
                relay_copy(relay).start()

        far = step - FAR_LAG

        @pl.when((far >= 0) & (far < steps) & has_far)
        def _():
            relay_copy(far).wait_recv()
            numerator, total = attend(q_far[far], far // SPLIT, bias_far)
            far_out[far] = numerator.astype(jnp.bfloat16)
            put_sum(far_sum, far, total)
            for one in far_copies(far):
                one.start()

        near = step - NEAR_LAG

        @pl.when((near >= 0) & (near < steps) & has_next)
        def _():
            numerator, total = attend(q_next[near], near // SPLIT, bias_near)

            @pl.when(has_prev)
            def _():
                for one in far_copies(near):
                    one.wait_recv()
                near_out[near] = (
                    numerator + far_in[near].astype(jnp.float32)
                ).astype(jnp.bfloat16)
                put_sum(near_sum, near, total + get_sum(far_sum_in, near))

            @pl.when(jnp.logical_not(has_prev))
            def _():
                near_out[near] = numerator.astype(jnp.bfloat16)
                put_sum(near_sum, near, total)

            for one in near_copies(near):
                one.start()

        own = step - OWN_LAG

        @pl.when((own >= 0) & (own < steps))
        def _():
            head, part = own // SPLIT, own % SPLIT
            numerator, total = attend(q_own[own], head, bias_own)
            place = pl.ds(pl.multiple_of(part * rows, rows), rows)
            stream = act_ref[0, place, lanes(head)].astype(jnp.float32)
            levels = gate_ref[0, :, lanes(head)]
            chosen = lax.broadcasted_iota(jnp.int32, levels.shape, 0) == level
            gate = jnp.sum(jnp.where(chosen, levels, 0.0), axis=0, keepdims=True)

            def finish(numerator, total):
                done[own] = (stream + numerator / total * gate).astype(jnp.bfloat16)

            @pl.when(has_prev)
            def _():
                for one in near_copies(own):
                    one.wait_recv()
                finish(
                    numerator + near_in[own].astype(jnp.float32),
                    total + get_sum(near_sum_in, own),
                )

            @pl.when(jnp.logical_not(has_prev))
            def _():
                finish(numerator, total)

            out_copy(own).start()

    @pl.loop(0, steps)
    def _(i):
        @pl.when(has_prev)
        def _():
            own_copy(i).wait_send()

        @pl.when(has_prev & has_next)
        def _():
            relay_copy(i).wait_send()

        @pl.when(has_far)
        def _():
            for one in far_copies(i):
                one.wait_send()

        @pl.when(has_next)
        def _():
            for one in near_copies(i):
                one.wait_send()

        out_copy(i).wait()


def body(spans, sections, activations, projected, noise_levels, frame_counts, span_mask, gates,
         norm_gains):
    tokens = activations.shape[1]
    heads, size = norm_gains.shape[2], norm_gains.shape[3]
    rows = tokens // SPLIT
    steps = heads * SPLIT
    wide = -(-rows // size) * size
    vmem = pl.BlockSpec(memory_space=pltpu.VMEM)
    smem = pl.BlockSpec(memory_space=pltpu.SMEM)
    piece = pltpu.VMEM((steps, rows, size), jnp.bfloat16)
    sums = pltpu.VMEM((steps, 1, wide), jnp.float32)
    work = 4 * heads * 3 * tokens * tokens * size
    return pl.pallas_call(
        functools.partial(kernel, spans, sections, steps),
        out_shape=jax.ShapeDtypeStruct(activations.shape, jnp.bfloat16),
        in_specs=[vmem, vmem, smem, smem, smem, vmem, vmem],
        out_specs=pl.BlockSpec(memory_space=pl.ANY),
        scratch_shapes=[
            piece,
            pltpu.VMEM((heads, tokens, size), jnp.bfloat16),
            pltpu.VMEM((heads, tokens, 2 * size), jnp.bfloat16),
            piece, piece, piece, sums, piece, sums, piece, sums, piece, sums, piece,
        ] + [pltpu.SemaphoreType.DMA((steps,))] * 14,
        compiler_params=pltpu.CompilerParams(
            collective_id=0, has_side_effects=True, vmem_limit_bytes=48 * 1024 * 1024
        ),
        cost_estimate=pl.CostEstimate(
            flops=work, bytes_accessed=5 * activations.size * 2,
            transcendentals=heads * 3 * tokens * tokens,
        ),
    )(activations, projected, noise_levels, frame_counts, span_mask, gates, norm_gains)


def solution(mesh):
    placed = (
        P("section", ("groups", "span"), "mp"),
        P("section", None, ("groups", "span"), "mp"),
        P("section", ("groups", "span")),
        P("section", "groups"),
        P("groups", None),
        P("section", None, "mp"),
        P("section", None, "mp", None),
    )
    return jax.shard_map(
        functools.partial(body, mesh.shape["span"], mesh.shape["section"]),
        mesh=mesh,
        in_specs=placed,
        out_specs=P("section", ("groups", "span"), "mp"),
        check_vma=False,
    )
```

```python
import functools
import math

import jax
import jax.numpy as jnp
from jax import lax
from jax.experimental import pallas as pl
from jax.experimental.pallas import tpu as pltpu
from jax.sharding import PartitionSpec as P

FRAMES = 16
EPSILON = 1e-06
MESH = pl.DeviceIdType.MESH
SPLIT = 2
RELAY_LAG, FAR_LAG, NEAR_LAG, OWN_LAG = 2, 4, 7, 10
MASKED = -1e30


def normalize(values, gain_row):
    values = values.astype(jnp.float32)
    mean_square = jnp.mean(values * values, axis=-1, keepdims=True)
    return (values * lax.rsqrt(mean_square + EPSILON) * gain_row).astype(jnp.bfloat16)


def kernel(
    spans, sections, steps,
    act_hbm, proj_hbm, noise_hbm, count_hbm, mask_hbm, gate_hbm, gain_hbm,
    out_ref,
    act_ref, proj_ref, noise_ref, count_ref, mask_ref, gate_ref, gain_ref,
    s_load, s_small,
    q_own, keys, vals, q_next, q_far, far_out, far_sum, far_in, far_sum_in,
    near_out, near_sum, near_in, near_sum_in, done,
    s_own, r_own, s_rel, r_rel, s_far, r_far, s_fars, r_fars,
    s_near, r_near, s_nears, r_nears, s_out, r_out,
):
    me = lax.axis_index("span")
    section = lax.axis_index("section")
    has_prev = me > 0
    has_next = me < spans - 1
    has_far = me < spans - 2
    prev_id = {"span": jnp.maximum(me - 1, 0)}
    next_id = {"span": jnp.minimum(me + 1, spans - 1)}
    out_id = {"section": lax.rem(section + 1, sections)}
    in_id = {"section": lax.rem(section + sections - 1, sections)}

    tokens = act_ref.shape[1]
    heads = gain_ref.shape[1]
    size = gain_ref.shape[3]
    rows = tokens // SPLIT
    scale = math.log2(math.e) / math.sqrt(size)
    tiles = [(lo, min(size, rows - lo)) for lo in range(0, rows, size)]

    barrier = pltpu.get_barrier_semaphore()
    pl.semaphore_signal(barrier, inc=1, device_id=out_id, device_id_type=MESH)
    pl.semaphore_signal(barrier, inc=1, device_id=in_id, device_id_type=MESH)

    @pl.when(has_prev)
    def _():
        pl.semaphore_signal(barrier, inc=1, device_id=prev_id, device_id_type=MESH)

    @pl.when(has_next)
    def _():
        pl.semaphore_signal(barrier, inc=1, device_id=next_id, device_id_type=MESH)

    def lanes(head):
        return pl.ds(pl.multiple_of(head * size, size), size)

    def load(kind, head):
        return pltpu.make_async_copy(
            proj_hbm.at[0, kind, :, lanes(head)],
            proj_ref.at[kind, :, lanes(head)],
            s_load.at[kind, head],
        )

    small = [
        pltpu.make_async_copy(src, dst, s_small.at[n])
        for n, (src, dst) in enumerate((
            (gain_hbm, gain_ref), (count_hbm, count_ref), (mask_hbm, mask_ref),
            (noise_hbm, noise_ref), (gate_hbm, gate_ref), (act_hbm, act_ref),
        ))
    ]
    load(0, 0).start()
    for one in small[:4]:
        one.start()

    @pl.loop(0, heads)
    def _(head):
        @pl.when(head > 0)
        def _():
            load(0, head).start()

        load(1, head).start()
        load(2, head).start()

    for one in small[4:]:
        one.start()
    for one in small[:4]:
        one.wait()

    token_row = lax.broadcasted_iota(jnp.int32, (1, tokens), 1)
    valid = token_row < count_ref[0, me] * (tokens // FRAMES)

    def bias_of(distance):
        allowed = mask_ref[jnp.minimum(me + distance, spans - 1), me]
        return jnp.where(valid & (allowed > 0), 0.0, MASKED)

    eye = lax.broadcasted_iota(jnp.int32, (size, size), 0) == lax.broadcasted_iota(
        jnp.int32, (size, size), 1
    )

    def prepare_query(head):
        load(0, head).wait()
        query = normalize(proj_ref[0, :, lanes(head)], gain_ref[0, head, 0:1])
        for part in range(SPLIT):
            q_own[head * SPLIT + part] = query[part * rows:(part + 1) * rows]

    def prepare_keys(head):
        load(1, head).wait()
        load(2, head).wait()
        keys[head] = normalize(proj_ref[1, :, lanes(head)], gain_ref[0, head, 1:2])
        vals[head, :, :size] = proj_ref[2, :, lanes(head)]
        vals[head, :, size:] = jnp.ones((tokens, size), jnp.bfloat16)

    prepare_query(0)

    def attend(query, head, bias):
        scores = lax.dot_general(
            query, keys[head], (((1,), (1,)), ((), ())),
            preferred_element_type=jnp.float32,
        )
        weights = jnp.exp2(scores * scale + bias).astype(jnp.bfloat16)
        both = jnp.dot(weights, vals[head], preferred_element_type=jnp.float32)
        return both[:, :size], both[:, size:]

    def put_sum(ref, index, total):
        for n, (lo, length) in enumerate(tiles):
            picked = jnp.where(eye[:length], total[lo:lo + length], 0.0)
            ref[index, :, n * size:(n + 1) * size] = jnp.sum(picked, axis=0, keepdims=True)

    def get_sum(ref, index):
        columns = []
        for n, (lo, length) in enumerate(tiles):
            row = ref[index, :, n * size:(n + 1) * size]
            picked = jnp.where(eye[:length], row, 0.0)
            columns.append(jnp.sum(picked, axis=1, keepdims=True))
        return jnp.concatenate(columns, axis=0)

    def copy(src, dst, send, recv, index, where):
        return pltpu.make_async_remote_copy(
            src_ref=src.at[index], dst_ref=dst.at[index],
            send_sem=send.at[index], recv_sem=recv.at[index],
            device_id=where, device_id_type=MESH,
        )

    def own_copy(i):
        return copy(q_own, q_next, s_own, r_own, i, prev_id)

    def relay_copy(i):
        return copy(q_next, q_far, s_rel, r_rel, i, prev_id)

    def far_copies(i):
        return (copy(far_out, far_in, s_far, r_far, i, next_id),
                copy(far_sum, far_sum_in, s_fars, r_fars, i, next_id))

    def near_copies(i):
        return (copy(near_out, near_in, s_near, r_near, i, next_id),
                copy(near_sum, near_sum_in, s_nears, r_nears, i, next_id))

    def out_copy(i):
        head, part = i // SPLIT, i % SPLIT
        place = pl.ds(pl.multiple_of(part * rows, rows), rows)
        return pltpu.make_async_remote_copy(
            src_ref=done.at[i], dst_ref=out_ref.at[0, place, lanes(head)],
            send_sem=s_out.at[i], recv_sem=r_out.at[i],
            device_id=out_id, device_id_type=MESH,
        )

    pl.semaphore_wait(
        barrier, 2 + has_prev.astype(jnp.int32) + has_next.astype(jnp.int32)
    )

    level = noise_ref[0, 0]
    for one in small[4:]:
        one.wait()
    bias_own, bias_near, bias_far = bias_of(0), bias_of(1), bias_of(2)

    @pl.loop(0, steps + OWN_LAG)
    def _(step):
        @pl.when((step < steps) & has_prev)
        def _():
            own_copy(step).start()

        @pl.when((step % SPLIT == SPLIT - 1) & (step < steps - 1))
        def _():
            prepare_query(step // SPLIT + 1)

        relay = step - RELAY_LAG

        @pl.when((relay >= 0) & (relay < steps) & has_next)
        def _():
            own_copy(relay).wait_recv()

            @pl.when(has_prev)
            def _():
                relay_copy(relay).start()

        far = step - FAR_LAG

        @pl.when((far >= 0) & (far < steps) & (far % SPLIT == 0))
        def _():
            prepare_keys(far // SPLIT)

        @pl.when((far >= 0) & (far < steps) & has_far)
        def _():
            relay_copy(far).wait_recv()
            numerator, total = attend(q_far[far], far // SPLIT, bias_far)
            far_out[far] = numerator.astype(jnp.bfloat16)
            put_sum(far_sum, far, total)
            for one in far_copies(far):
                one.start()

        near = step - NEAR_LAG

        @pl.when((near >= 0) & (near < steps) & has_next)
        def _():
            numerator, total = attend(q_next[near], near // SPLIT, bias_near)

            @pl.when(has_prev)
            def _():
                for one in far_copies(near):
                    one.wait_recv()
                near_out[near] = (
                    numerator + far_in[near].astype(jnp.float32)
                ).astype(jnp.bfloat16)
                put_sum(near_sum, near, total + get_sum(far_sum_in, near))

            @pl.when(jnp.logical_not(has_prev))
            def _():
                near_out[near] = numerator.astype(jnp.bfloat16)
                put_sum(near_sum, near, total)

            for one in near_copies(near):
                one.start()

        own = step - OWN_LAG

        @pl.when((own >= 0) & (own < steps))
        def _():
            head, part = own // SPLIT, own % SPLIT
            numerator, total = attend(q_own[own], head, bias_own)
            place = pl.ds(pl.multiple_of(part * rows, rows), rows)
            stream = act_ref[0, place, lanes(head)].astype(jnp.float32)
            levels = gate_ref[0, :, lanes(head)]
            chosen = lax.broadcasted_iota(jnp.int32, levels.shape, 0) == level
            gate = jnp.sum(jnp.where(chosen, levels, 0.0), axis=0, keepdims=True)

            def finish(numerator, total):
                done[own] = (stream + numerator / total * gate).astype(jnp.bfloat16)

            @pl.when(has_prev)
            def _():
                for one in near_copies(own):
                    one.wait_recv()
                finish(
                    numerator + near_in[own].astype(jnp.float32),
                    total + get_sum(near_sum_in, own),
                )

            @pl.when(jnp.logical_not(has_prev))
            def _():
                finish(numerator, total)

            out_copy(own).start()

            @pl.when(has_prev)
            def _():
                own_copy(own).wait_send()

            @pl.when(has_prev & has_next)
            def _():
                relay_copy(own).wait_send()

            @pl.when(has_far)
            def _():
                for one in far_copies(own):
                    one.wait_send()

            @pl.when(has_next)
            def _():
                for one in near_copies(own):
                    one.wait_send()

    @pl.loop(0, steps)
    def _(i):
        out_copy(i).wait()


def body(spans, sections, activations, projected, noise_levels, frame_counts, span_mask, gates,
         norm_gains):
    tokens = activations.shape[1]
    heads, size = norm_gains.shape[2], norm_gains.shape[3]
    rows = tokens // SPLIT
    steps = heads * SPLIT
    wide = -(-rows // size) * size
    hbm = pl.BlockSpec(memory_space=pltpu.HBM)
    swapped_gains = jnp.transpose(norm_gains, (0, 2, 1, 3))
    piece = pltpu.VMEM((steps, rows, size), jnp.bfloat16)
    sums = pltpu.VMEM((steps, 1, wide), jnp.float32)
    work = 4 * heads * 3 * tokens * tokens * size
    return pl.pallas_call(
        functools.partial(kernel, spans, sections, steps),
        out_shape=jax.ShapeDtypeStruct(activations.shape, jnp.bfloat16),
        in_specs=[hbm] * 7,
        out_specs=pl.BlockSpec(memory_space=pl.ANY),
        scratch_shapes=[
            pltpu.VMEM(activations.shape, jnp.bfloat16),
            pltpu.VMEM(projected.shape[1:], jnp.bfloat16),
            pltpu.SMEM(noise_levels.shape, jnp.int32),
            pltpu.SMEM(frame_counts.shape, jnp.int32),
            pltpu.SMEM(span_mask.shape, jnp.int32),
            pltpu.VMEM(gates.shape, jnp.float32),
            pltpu.VMEM(swapped_gains.shape, jnp.float32),
            pltpu.SemaphoreType.DMA((3, heads)),
            pltpu.SemaphoreType.DMA((6,)),
            piece,
            pltpu.VMEM((heads, tokens, size), jnp.bfloat16),
            pltpu.VMEM((heads, tokens, 2 * size), jnp.bfloat16),
            piece, piece, piece, sums, piece, sums, piece, sums, piece, sums, piece,
        ] + [pltpu.SemaphoreType.DMA((steps,))] * 14,
        compiler_params=pltpu.CompilerParams(
            collective_id=0, has_side_effects=True, vmem_limit_bytes=62 * 1024 * 1024
        ),
        cost_estimate=pl.CostEstimate(
            flops=work, bytes_accessed=5 * activations.size * 2,
            transcendentals=heads * 3 * tokens * tokens,
        ),
    )(activations, projected, noise_levels, frame_counts, span_mask, gates, swapped_gains)


def solution(mesh):
    placed = (
        P("section", ("groups", "span"), "mp"),
        P("section", None, ("groups", "span"), "mp"),
        P("section", ("groups", "span")),
        P("section", "groups"),
        P("groups", None),
        P("section", None, "mp"),
        P("section", None, "mp", None),
    )
    return jax.shard_map(
        functools.partial(body, mesh.shape["span"], mesh.shape["section"]),
        mesh=mesh,
        in_specs=placed,
        out_specs=P("section", ("groups", "span"), "mp"),
        check_vma=False,
    )
```

```python
import functools
import math

import jax
import jax.numpy as jnp
from jax import lax
from jax.experimental import pallas as pl
from jax.experimental.pallas import tpu as pltpu
from jax.sharding import PartitionSpec as P

FRAMES = 16
EPSILON = 1e-06
MESH = pl.DeviceIdType.MESH
SPLIT = 1
RELAY_LAG, FAR_LAG, NEAR_LAG, OWN_LAG = 1, 2, 4, 6
MASKED = -1e30


def normalize(values, gain_row):
    values = values.astype(jnp.float32)
    mean_square = jnp.mean(values * values, axis=-1, keepdims=True)
    return (values * lax.rsqrt(mean_square + EPSILON) * gain_row).astype(jnp.bfloat16)


def kernel(
    spans, sections, steps,
    act_hbm, proj_hbm, noise_hbm, count_hbm, mask_hbm, gate_hbm, gain_hbm,
    out_ref,
    act_ref, proj_ref, noise_ref, count_ref, mask_ref, gate_ref, gain_ref,
    s_load, s_small,
    q_own, keys, vals, q_next, q_far, far_out, far_sum, far_in, far_sum_in,
    near_out, near_sum, near_in, near_sum_in, done,
    s_own, r_own, s_rel, r_rel, s_far, r_far, s_fars, r_fars,
    s_near, r_near, s_nears, r_nears, s_out, r_out,
):
    me = lax.axis_index("span")
    section = lax.axis_index("section")
    has_prev = me > 0
    has_next = me < spans - 1
    has_far = me < spans - 2
    prev_id = {"span": jnp.maximum(me - 1, 0)}
    next_id = {"span": jnp.minimum(me + 1, spans - 1)}
    out_id = {"section": lax.rem(section + 1, sections)}
    in_id = {"section": lax.rem(section + sections - 1, sections)}

    tokens = act_ref.shape[1]
    heads = gain_ref.shape[1]
    size = gain_ref.shape[3]
    rows = tokens // SPLIT
    scale = math.log2(math.e) / math.sqrt(size)
    tiles = [(lo, min(size, rows - lo)) for lo in range(0, rows, size)]

    barrier = pltpu.get_barrier_semaphore()
    pl.semaphore_signal(barrier, inc=1, device_id=out_id, device_id_type=MESH)
    pl.semaphore_signal(barrier, inc=1, device_id=in_id, device_id_type=MESH)

    @pl.when(has_prev)
    def _():
        pl.semaphore_signal(barrier, inc=1, device_id=prev_id, device_id_type=MESH)

    @pl.when(has_next)
    def _():
        pl.semaphore_signal(barrier, inc=1, device_id=next_id, device_id_type=MESH)

    def lanes(head):
        return pl.ds(pl.multiple_of(head * size, size), size)

    def load(kind, head):
        return pltpu.make_async_copy(
            proj_hbm.at[0, kind, :, lanes(head)],
            proj_ref.at[kind, :, lanes(head)],
            s_load.at[kind, head],
        )

    small = [
        pltpu.make_async_copy(src, dst, s_small.at[n])
        for n, (src, dst) in enumerate((
            (gain_hbm, gain_ref), (count_hbm, count_ref), (mask_hbm, mask_ref),
            (noise_hbm, noise_ref), (gate_hbm, gate_ref), (act_hbm, act_ref),
        ))
    ]
    load(0, 0).start()
    for one in small[:4]:
        one.start()

    @pl.loop(0, heads)
    def _(head):
        @pl.when(head > 0)
        def _():
            load(0, head).start()

        load(1, head).start()
        load(2, head).start()

    for one in small[4:]:
        one.start()
    for one in small[:4]:
        one.wait()

    token_row = lax.broadcasted_iota(jnp.int32, (1, tokens), 1)
    valid = token_row < count_ref[0, me] * (tokens // FRAMES)

    def bias_of(distance):
        allowed = mask_ref[jnp.minimum(me + distance, spans - 1), me]
        return jnp.where(valid & (allowed > 0), 0.0, MASKED)

    eye = lax.broadcasted_iota(jnp.int32, (size, size), 0) == lax.broadcasted_iota(
        jnp.int32, (size, size), 1
    )

    def prepare_query(head):
        load(0, head).wait()
        query = normalize(proj_ref[0, :, lanes(head)], gain_ref[0, head, 0:1])
        for part in range(SPLIT):
            q_own[head * SPLIT + part] = query[part * rows:(part + 1) * rows]

    def prepare_keys(head):
        load(1, head).wait()
        load(2, head).wait()
        keys[head] = normalize(proj_ref[1, :, lanes(head)], gain_ref[0, head, 1:2])
        vals[head, :, :size] = proj_ref[2, :, lanes(head)]
        vals[head, :, size:] = jnp.ones((tokens, size), jnp.bfloat16)

    prepare_query(0)

    def attend(query, head, bias):
        scores = lax.dot_general(
            query, keys[head], (((1,), (1,)), ((), ())),
            preferred_element_type=jnp.float32,
        )
        weights = jnp.exp2(scores * scale + bias).astype(jnp.bfloat16)
        both = jnp.dot(weights, vals[head], preferred_element_type=jnp.float32)
        return both[:, :size], both[:, size:]

    def put_sum(ref, index, total):
        for n, (lo, length) in enumerate(tiles):
            picked = jnp.where(eye[:length], total[lo:lo + length], 0.0)
            ref[index, :, n * size:(n + 1) * size] = jnp.sum(picked, axis=0, keepdims=True)

    def get_sum(ref, index):
        columns = []
        for n, (lo, length) in enumerate(tiles):
            row = ref[index, :, n * size:(n + 1) * size]
            picked = jnp.where(eye[:length], row, 0.0)
            columns.append(jnp.sum(picked, axis=1, keepdims=True))
        return jnp.concatenate(columns, axis=0)

    def copy(src, dst, send, recv, index, where):
        return pltpu.make_async_remote_copy(
            src_ref=src.at[index], dst_ref=dst.at[index],
            send_sem=send.at[index], recv_sem=recv.at[index],
            device_id=where, device_id_type=MESH,
        )

    def own_copy(i):
        return copy(q_own, q_next, s_own, r_own, i, prev_id)

    def relay_copy(i):
        return copy(q_next, q_far, s_rel, r_rel, i, prev_id)

    def far_copies(i):
        return (copy(far_out, far_in, s_far, r_far, i, next_id),
                copy(far_sum, far_sum_in, s_fars, r_fars, i, next_id))

    def near_copies(i):
        return (copy(near_out, near_in, s_near, r_near, i, next_id),
                copy(near_sum, near_sum_in, s_nears, r_nears, i, next_id))

    def out_copy(i):
        head, part = i // SPLIT, i % SPLIT
        place = pl.ds(pl.multiple_of(part * rows, rows), rows)
        return pltpu.make_async_remote_copy(
            src_ref=done.at[i], dst_ref=out_ref.at[0, place, lanes(head)],
            send_sem=s_out.at[i], recv_sem=r_out.at[i],
            device_id=out_id, device_id_type=MESH,
        )

    pl.semaphore_wait(
        barrier, 2 + has_prev.astype(jnp.int32) + has_next.astype(jnp.int32)
    )

    level = noise_ref[0, 0]
    for one in small[4:]:
        one.wait()
    bias_own, bias_near, bias_far = bias_of(0), bias_of(1), bias_of(2)

    @pl.loop(0, steps + OWN_LAG)
    def _(step):
        @pl.when((step < steps) & has_prev)
        def _():
            own_copy(step).start()

        @pl.when((step % SPLIT == SPLIT - 1) & (step < steps - 1))
        def _():
            prepare_query(step // SPLIT + 1)

        relay = step - RELAY_LAG

        @pl.when((relay >= 0) & (relay < steps) & has_next)
        def _():
            own_copy(relay).wait_recv()

            @pl.when(has_prev)
            def _():
                relay_copy(relay).start()

        far = step - FAR_LAG

        @pl.when((far >= 0) & (far < steps) & (far % SPLIT == 0))
        def _():
            prepare_keys(far // SPLIT)

        @pl.when((far >= 0) & (far < steps) & has_far)
        def _():
            relay_copy(far).wait_recv()
            numerator, total = attend(q_far[far], far // SPLIT, bias_far)
            far_out[far] = numerator.astype(jnp.bfloat16)
            put_sum(far_sum, far, total)
            for one in far_copies(far):
                one.start()

        near = step - NEAR_LAG

        @pl.when((near >= 0) & (near < steps) & has_next)
        def _():
            numerator, total = attend(q_next[near], near // SPLIT, bias_near)

            @pl.when(has_prev)
            def _():
                for one in far_copies(near):
                    one.wait_recv()
                near_out[near] = (
                    numerator + far_in[near].astype(jnp.float32)
                ).astype(jnp.bfloat16)
                put_sum(near_sum, near, total + get_sum(far_sum_in, near))

            @pl.when(jnp.logical_not(has_prev))
            def _():
                near_out[near] = numerator.astype(jnp.bfloat16)
                put_sum(near_sum, near, total)

            for one in near_copies(near):
                one.start()

        own = step - OWN_LAG

        @pl.when((own >= 0) & (own < steps))
        def _():
            head, part = own // SPLIT, own % SPLIT
            numerator, total = attend(q_own[own], head, bias_own)
            place = pl.ds(pl.multiple_of(part * rows, rows), rows)
            stream = act_ref[0, place, lanes(head)].astype(jnp.float32)
            levels = gate_ref[0, :, lanes(head)]
            chosen = lax.broadcasted_iota(jnp.int32, levels.shape, 0) == level
            gate = jnp.sum(jnp.where(chosen, levels, 0.0), axis=0, keepdims=True)

            def finish(numerator, total):
                done[own] = (stream + numerator / total * gate).astype(jnp.bfloat16)

            @pl.when(has_prev)
            def _():
                for one in near_copies(own):
                    one.wait_recv()
                finish(
                    numerator + near_in[own].astype(jnp.float32),
                    total + get_sum(near_sum_in, own),
                )

            @pl.when(jnp.logical_not(has_prev))
            def _():
                finish(numerator, total)

            out_copy(own).start()

            @pl.when(has_prev)
            def _():
                own_copy(own).wait_send()

            @pl.when(has_prev & has_next)
            def _():
                relay_copy(own).wait_send()

            @pl.when(has_far)
            def _():
                for one in far_copies(own):
                    one.wait_send()

            @pl.when(has_next)
            def _():
                for one in near_copies(own):
                    one.wait_send()

    @pl.loop(0, steps)
    def _(i):
        out_copy(i).wait()


def body(spans, sections, activations, projected, noise_levels, frame_counts, span_mask, gates,
         norm_gains):
    tokens = activations.shape[1]
    heads, size = norm_gains.shape[2], norm_gains.shape[3]
    rows = tokens // SPLIT
    steps = heads * SPLIT
    wide = -(-rows // size) * size
    hbm = pl.BlockSpec(memory_space=pltpu.HBM)
    swapped_gains = jnp.transpose(norm_gains, (0, 2, 1, 3))
    piece = pltpu.VMEM((steps, rows, size), jnp.bfloat16)
    sums = pltpu.VMEM((steps, 1, wide), jnp.float32)
    work = 4 * heads * 3 * tokens * tokens * size
    return pl.pallas_call(
        functools.partial(kernel, spans, sections, steps),
        out_shape=jax.ShapeDtypeStruct(activations.shape, jnp.bfloat16),
        in_specs=[hbm] * 7,
        out_specs=pl.BlockSpec(memory_space=pl.ANY),
        scratch_shapes=[
            pltpu.VMEM(activations.shape, jnp.bfloat16),
            pltpu.VMEM(projected.shape[1:], jnp.bfloat16),
            pltpu.SMEM(noise_levels.shape, jnp.int32),
            pltpu.SMEM(frame_counts.shape, jnp.int32),
            pltpu.SMEM(span_mask.shape, jnp.int32),
            pltpu.VMEM(gates.shape, jnp.float32),
            pltpu.VMEM(swapped_gains.shape, jnp.float32),
            pltpu.SemaphoreType.DMA((3, heads)),
            pltpu.SemaphoreType.DMA((6,)),
            piece,
            pltpu.VMEM((heads, tokens, size), jnp.bfloat16),
            pltpu.VMEM((heads, tokens, 2 * size), jnp.bfloat16),
            piece, piece, piece, sums, piece, sums, piece, sums, piece, sums, piece,
        ] + [pltpu.SemaphoreType.DMA((steps,))] * 14,
        compiler_params=pltpu.CompilerParams(
            collective_id=0, has_side_effects=True, vmem_limit_bytes=62 * 1024 * 1024
        ),
        cost_estimate=pl.CostEstimate(
            flops=work, bytes_accessed=5 * activations.size * 2,
            transcendentals=heads * 3 * tokens * tokens,
        ),
    )(activations, projected, noise_levels, frame_counts, span_mask, gates, swapped_gains)


def solution(mesh):
    placed = (
        P("section", ("groups", "span"), "mp"),
        P("section", None, ("groups", "span"), "mp"),
        P("section", ("groups", "span")),
        P("section", "groups"),
        P("groups", None),
        P("section", None, "mp"),
        P("section", None, "mp", None),
    )
    return jax.shard_map(
        functools.partial(body, mesh.shape["span"], mesh.shape["section"]),
        mesh=mesh,
        in_specs=placed,
        out_specs=P("section", ("groups", "span"), "mp"),
        check_vma=False,
    )
```

```python
import functools
import math

import jax
import jax.numpy as jnp
from jax import lax
from jax.experimental import pallas as pl
from jax.experimental.pallas import tpu as pltpu
from jax.sharding import PartitionSpec as P

FRAMES = 16
EPSILON = 1e-06
MESH = pl.DeviceIdType.MESH
SPLIT = 1
RELAY_LAG, FAR_LAG, NEAR_LAG, OWN_LAG = 1, 2, 4, 6
MASKED = -1e30


def normalize(values, gain_row):
    values = values.astype(jnp.float32)
    mean_square = jnp.mean(values * values, axis=-1, keepdims=True)
    return (values * lax.rsqrt(mean_square + EPSILON) * gain_row).astype(jnp.bfloat16)


def kernel(
    spans, sections, steps,
    act_hbm, proj_hbm, noise_hbm, count_hbm, mask_hbm, gate_hbm, gain_hbm,
    out_ref,
    act_ref, proj_ref, noise_ref, count_ref, mask_ref, gate_ref, gain_ref,
    s_load, s_small,
    q_own, keys, vals, q_next, q_far, far_out, far_sum, far_in, far_sum_in,
    near_out, near_sum, near_in, near_sum_in, done,
    s_own, r_own, s_rel, r_rel, s_far, r_far, s_fars, r_fars,
    s_near, r_near, s_nears, r_nears, s_out, r_out,
):
    me = lax.axis_index("span")
    section = lax.axis_index("section")
    has_prev = me > 0
    has_next = me < spans - 1
    has_far = me < spans - 2
    prev_id = {"span": jnp.maximum(me - 1, 0)}
    next_id = {"span": jnp.minimum(me + 1, spans - 1)}
    out_id = {"section": lax.rem(section + 1, sections)}
    in_id = {"section": lax.rem(section + sections - 1, sections)}

    tokens = act_ref.shape[1]
    heads = gain_ref.shape[1]
    size = gain_ref.shape[3]
    rows = tokens // SPLIT
    scale = math.log2(math.e) / math.sqrt(size)
    tiles = [(lo, min(size, rows - lo)) for lo in range(0, rows, size)]

    barrier = pltpu.get_barrier_semaphore()
    pl.semaphore_signal(barrier, inc=1, device_id=out_id, device_id_type=MESH)
    pl.semaphore_signal(barrier, inc=1, device_id=in_id, device_id_type=MESH)

    @pl.when(has_prev)
    def _():
        pl.semaphore_signal(barrier, inc=1, device_id=prev_id, device_id_type=MESH)

    @pl.when(has_next)
    def _():
        pl.semaphore_signal(barrier, inc=1, device_id=next_id, device_id_type=MESH)

    def lanes(head):
        return pl.ds(pl.multiple_of(head * size, size), size)

    def load(kind, head):
        return pltpu.make_async_copy(
            proj_hbm.at[0, kind, :, lanes(head)],
            proj_ref.at[kind, :, lanes(head)],
            s_load.at[kind, head],
        )

    small = [
        pltpu.make_async_copy(src, dst, s_small.at[n])
        for n, (src, dst) in enumerate((
            (gain_hbm, gain_ref), (count_hbm, count_ref), (mask_hbm, mask_ref),
            (noise_hbm, noise_ref), (gate_hbm, gate_ref), (act_hbm, act_ref),
        ))
    ]
    load(0, 0).start()
    for one in small[:4]:
        one.start()

    @pl.loop(0, heads)
    def _(head):
        @pl.when(head > 0)
        def _():
            load(0, head).start()

        load(1, head).start()
        load(2, head).start()

    for one in small[4:]:
        one.start()
    for one in small[:4]:
        one.wait()

    token_row = lax.broadcasted_iota(jnp.int32, (1, tokens), 1)
    valid = token_row < count_ref[0, me] * (tokens // FRAMES)

    def bias_of(distance):
        allowed = mask_ref[jnp.minimum(me + distance, spans - 1), me]
        return jnp.where(valid & (allowed > 0), 0.0, MASKED)

    eye = lax.broadcasted_iota(jnp.int32, (size, size), 0) == lax.broadcasted_iota(
        jnp.int32, (size, size), 1
    )

    def prepare_query(head):
        load(0, head).wait()
        query = normalize(proj_ref[0, :, lanes(head)], gain_ref[0, head, 0:1])
        for part in range(SPLIT):
            q_own[head * SPLIT + part] = query[part * rows:(part + 1) * rows]

    def prepare_keys(head):
        load(1, head).wait()
        load(2, head).wait()
        keys[head] = normalize(proj_ref[1, :, lanes(head)], gain_ref[0, head, 1:2])
        vals[head, :, :size] = proj_ref[2, :, lanes(head)]
        vals[head, :, size:] = jnp.ones((tokens, size), jnp.bfloat16)

    prepare_query(0)

    def attend(query, head, bias):
        scores = lax.dot_general(
            query, keys[head], (((1,), (1,)), ((), ())),
            preferred_element_type=jnp.float32,
        )
        weights = jnp.exp2(scores * scale + bias).astype(jnp.bfloat16)
        both = jnp.dot(weights, vals[head], preferred_element_type=jnp.float32)
        return both[:, :size], both[:, size:]

    def put_sum(ref, index, total):
        for n, (lo, length) in enumerate(tiles):
            picked = jnp.where(eye[:length], total[lo:lo + length], 0.0)
            ref[index, :, n * size:(n + 1) * size] = jnp.sum(picked, axis=0, keepdims=True)

    def get_sum(ref, index):
        columns = []
        for n, (lo, length) in enumerate(tiles):
            row = ref[index, :, n * size:(n + 1) * size]
            picked = jnp.where(eye[:length], row, 0.0)
            columns.append(jnp.sum(picked, axis=1, keepdims=True))
        return jnp.concatenate(columns, axis=0)

    def copy(src, dst, send, recv, index, where):
        return pltpu.make_async_remote_copy(
            src_ref=src.at[index], dst_ref=dst.at[index],
            send_sem=send.at[index], recv_sem=recv.at[index],
            device_id=where, device_id_type=MESH,
        )

    def own_copy(i):
        return copy(q_own, q_next, s_own, r_own, i, prev_id)

    def relay_copy(i):
        return copy(q_next, q_far, s_rel, r_rel, i, prev_id)

    def far_copies(i):
        return (copy(far_out, far_in, s_far, r_far, i, next_id),
                copy(far_sum, far_sum_in, s_fars, r_fars, i, next_id))

    def near_copies(i):
        return (copy(near_out, near_in, s_near, r_near, i, next_id),
                copy(near_sum, near_sum_in, s_nears, r_nears, i, next_id))

    def out_copy(i):
        head, part = i // SPLIT, i % SPLIT
        place = pl.ds(pl.multiple_of(part * rows, rows), rows)
        return pltpu.make_async_remote_copy(
            src_ref=done.at[i], dst_ref=out_ref.at[0, place, lanes(head)],
            send_sem=s_out.at[i], recv_sem=r_out.at[i],
            device_id=out_id, device_id_type=MESH,
        )

    pl.semaphore_wait(
        barrier, 2 + has_prev.astype(jnp.int32) + has_next.astype(jnp.int32)
    )

    level = noise_ref[0, 0]
    for one in small[4:]:
        one.wait()
    bias_own, bias_near, bias_far = bias_of(0), bias_of(1), bias_of(2)

    @pl.loop(0, steps + OWN_LAG)
    def _(step):
        @pl.when((step < steps) & has_prev)
        def _():
            own_copy(step).start()

        @pl.when((step % SPLIT == SPLIT - 1) & (step < steps - 1))
        def _():
            prepare_query(step // SPLIT + 1)

        own = step - OWN_LAG

        @pl.when((own >= 0) & (own < steps))
        def _():
            head, part = own // SPLIT, own % SPLIT
            numerator, total = attend(q_own[own], head, bias_own)
            place = pl.ds(pl.multiple_of(part * rows, rows), rows)
            stream = act_ref[0, place, lanes(head)].astype(jnp.float32)
            levels = gate_ref[0, :, lanes(head)]
            chosen = lax.broadcasted_iota(jnp.int32, levels.shape, 0) == level
            gate = jnp.sum(jnp.where(chosen, levels, 0.0), axis=0, keepdims=True)

            def finish(numerator, total):
                done[own] = (stream + numerator / total * gate).astype(jnp.bfloat16)

            @pl.when(has_prev)
            def _():
                for one in near_copies(own):
                    one.wait_recv()
                finish(
                    numerator + near_in[own].astype(jnp.float32),
                    total + get_sum(near_sum_in, own),
                )

            @pl.when(jnp.logical_not(has_prev))
            def _():
                finish(numerator, total)

            out_copy(own).start()

            @pl.when(has_prev)
            def _():
                own_copy(own).wait_send()

            @pl.when(has_prev & has_next)
            def _():
                relay_copy(own).wait_send()

            @pl.when(has_far)
            def _():
                for one in far_copies(own):
                    one.wait_send()

            @pl.when(has_next)
            def _():
                for one in near_copies(own):
                    one.wait_send()

        relay = step - RELAY_LAG

        @pl.when((relay >= 0) & (relay < steps) & has_next)
        def _():
            own_copy(relay).wait_recv()

            @pl.when(has_prev)
            def _():
                relay_copy(relay).start()

        far = step - FAR_LAG

        @pl.when((far >= 0) & (far < steps) & (far % SPLIT == 0))
        def _():
            prepare_keys(far // SPLIT)

        @pl.when((far >= 0) & (far < steps) & has_far)
        def _():
            relay_copy(far).wait_recv()
            numerator, total = attend(q_far[far], far // SPLIT, bias_far)
            far_out[far] = numerator.astype(jnp.bfloat16)
            put_sum(far_sum, far, total)
            for one in far_copies(far):
                one.start()

        near = step - NEAR_LAG

        @pl.when((near >= 0) & (near < steps) & has_next)
        def _():
            numerator, total = attend(q_next[near], near // SPLIT, bias_near)

            @pl.when(has_prev)
            def _():
                for one in far_copies(near):
                    one.wait_recv()
                near_out[near] = (
                    numerator + far_in[near].astype(jnp.float32)
                ).astype(jnp.bfloat16)
                put_sum(near_sum, near, total + get_sum(far_sum_in, near))

            @pl.when(jnp.logical_not(has_prev))
            def _():
                near_out[near] = numerator.astype(jnp.bfloat16)
                put_sum(near_sum, near, total)

            for one in near_copies(near):
                one.start()

    @pl.loop(0, steps)
    def _(i):
        out_copy(i).wait()


def body(spans, sections, activations, projected, noise_levels, frame_counts, span_mask, gates,
         norm_gains):
    tokens = activations.shape[1]
    heads, size = norm_gains.shape[2], norm_gains.shape[3]
    rows = tokens // SPLIT
    steps = heads * SPLIT
    wide = -(-rows // size) * size
    hbm = pl.BlockSpec(memory_space=pltpu.HBM)
    swapped_gains = jnp.transpose(norm_gains, (0, 2, 1, 3))
    piece = pltpu.VMEM((steps, rows, size), jnp.bfloat16)
    sums = pltpu.VMEM((steps, 1, wide), jnp.float32)
    work = 4 * heads * 3 * tokens * tokens * size
    return pl.pallas_call(
        functools.partial(kernel, spans, sections, steps),
        out_shape=jax.ShapeDtypeStruct(activations.shape, jnp.bfloat16),
        in_specs=[hbm] * 7,
        out_specs=pl.BlockSpec(memory_space=pl.ANY),
        scratch_shapes=[
            pltpu.VMEM(activations.shape, jnp.bfloat16),
            pltpu.VMEM(projected.shape[1:], jnp.bfloat16),
            pltpu.SMEM(noise_levels.shape, jnp.int32),
            pltpu.SMEM(frame_counts.shape, jnp.int32),
            pltpu.SMEM(span_mask.shape, jnp.int32),
            pltpu.VMEM(gates.shape, jnp.float32),
            pltpu.VMEM(swapped_gains.shape, jnp.float32),
            pltpu.SemaphoreType.DMA((3, heads)),
            pltpu.SemaphoreType.DMA((6,)),
            piece,
            pltpu.VMEM((heads, tokens, size), jnp.bfloat16),
            pltpu.VMEM((heads, tokens, 2 * size), jnp.bfloat16),
            piece, piece, piece, sums, piece, sums, piece, sums, piece, sums, piece,
        ] + [pltpu.SemaphoreType.DMA((steps,))] * 14,
        compiler_params=pltpu.CompilerParams(
            collective_id=0, has_side_effects=True, vmem_limit_bytes=62 * 1024 * 1024
        ),
        cost_estimate=pl.CostEstimate(
            flops=work, bytes_accessed=5 * activations.size * 2,
            transcendentals=heads * 3 * tokens * tokens,
        ),
    )(activations, projected, noise_levels, frame_counts, span_mask, gates, swapped_gains)


def solution(mesh):
    placed = (
        P("section", ("groups", "span"), "mp"),
        P("section", None, ("groups", "span"), "mp"),
        P("section", ("groups", "span")),
        P("section", "groups"),
        P("groups", None),
        P("section", None, "mp"),
        P("section", None, "mp", None),
    )
    return jax.shard_map(
        functools.partial(body, mesh.shape["span"], mesh.shape["section"]),
        mesh=mesh,
        in_specs=placed,
        out_specs=P("section", ("groups", "span"), "mp"),
        check_vma=False,
    )
```
